128 devices in a mesh: row: 16 (over y, x_lo, core), col: 8 (over z, x_hi).
Axes of the slice: x: 4 (x_hi: 2, x_lo: 2; x = x_hi * 2 + x_lo), y: 4, z: 4, core: 2. Of those that a mesh axis runs over, the one named last changes fastest.
Arguments:
- grad: float32 [4096, 6144], P('row', 'col'), may hold values from -6 to 6
- weight: float32 [4096, 6144], P('row', 'col'), may hold values from -6 to 6
- exp_avg: float32 [4096, 6144], P('row', 'col'), may hold values from -2 to 2
- exp_avg_sq: float32 [4096, 6144], P('row', 'col'), may hold values from 0.05 to 3
- left_basis: bfloat16 [4096, 4096], P('row', 'col'), may hold values from -0.125 to 0.125
- right_basis: bfloat16 [6144, 6144], P('col', 'row'), may hold values from -0.109375 to 0.109375
Outputs:
- new_weight: float32 [4096, 6144], P('row', 'col')
- new_avg: float32 [4096, 6144], P('row', 'col')
- new_avg_sq: float32 [4096, 6144], P('row', 'col')
The draws below stay inside these ranges and needn't reach their ends.
All inputs are finite; a program needn't handle non-finite values.
Results may differ from the reference program's by a relative error of at most 0.014.
Values may be sent and summed in bfloat16 or wider, within the bound.
No kernel may reach another device: no remote copies, remote signals or barrier semaphores. Data moves between devices by JAX's collectives and lax.ppermute only.
A program may use at most 64 MiB of HBM per device.

```python
import math
import jax
import jax.numpy as jnp
from jax import lax

D = 4096
N = 6144
N_ROW = 16
N_COL = 8


def spiked(array, key, source, target, blocks, factor):
    owner, partner = [(jnp.arange(array.shape[position]) // (array.shape[position] // blocks)).reshape([-1 if axis == position else 1 for axis in range(array.ndim)]) for position in (source, target)]
    chosen = jax.random.permutation(key, blocks)[partner]
    strong = (owner == chosen) | (owner == (partner + blocks // 2) % blocks)
    return jnp.where(strong, factor * array, array)


def shard_levels(key, dims, cuts, least, largest):
    factor_of, own = 1.0, jax.random.fold_in(key, 6)
    for dim, blocks in cuts:
        steps = jnp.exp(jax.random.uniform(jax.random.fold_in(own, dim), (blocks,), jnp.float32, least / len(cuts), largest / len(cuts)))
        factor_of = factor_of * jnp.repeat(steps, dims[dim] // blocks).reshape([-1 if axis == dim else 1 for axis in range(len(dims))])
    return factor_of


def gaussian(rng, extent, width, bound, split=(), held_as=jnp.bfloat16):
    array = width * jax.random.normal(rng, extent, jnp.float32)
    if split:
        array = array * shard_levels(rng, extent, split, -0.22, 0.18)
    return jnp.clip(array, -bound, bound).astype(held_as)


def gaussian_with(own_key, extent, scale, bound, cuts, heavy, held_as=jnp.bfloat16):
    entries = scale * jax.random.normal(own_key, extent, jnp.float32)
    if cuts:
        entries = entries * shard_levels(own_key, extent, cuts, -0.22, 0.18)
    return jnp.clip(spiked(entries, jax.random.fold_in(own_key, 3), *heavy), -bound, bound).astype(held_as)


def setup_inputs(seed: int = 0) -> dict:
    keys = jax.random.split(jax.random.key(seed), 7)
    grad = gaussian(keys[0], (D, N), 1.0, 6.0, ((0, 16), (1, 8)), jnp.float32)
    weight = gaussian(keys[1], (D, N), 1.0, 6.0, ((0, 16), (1, 8)), jnp.float32)
    exp_avg = gaussian(keys[2], (D, N), 0.3, 2.0, ((0, 16), (1, 8)), jnp.float32)
    exp_avg_sq = jnp.clip(jnp.exp(math.log(3.0) - 4.0943445 * jax.random.uniform(keys[3], (D, N), jnp.float32) ** shard_levels(keys[3], (D, N), ((0, 16), (1, 8)), -0.2, 0.2)), 0.05, 3.0)
    left_basis = gaussian_with(keys[4], (D, D), D ** -0.5, 0.125, ((0, 16), (1, 8)), (0, 1, 16, 2.0))
    right_basis = gaussian_with(keys[5], (N, N), N ** -0.5, 0.109375, ((0, 8), (1, 16)), (0, 1, 16, 2.0))
    return dict(grad=grad, weight=weight, exp_avg=exp_avg, exp_avg_sq=exp_avg_sq, left_basis=left_basis, right_basis=right_basis)


first_beta = 0.9
second_beta = 0.95
first_bias = 1.0 - 0.9 ** 20
second_bias = 1.0 - 0.95 ** 20
epsilon = 1e-08
learn_rate = 0.2
weight_decay = 0.1

def rounded_add(total, part):
    low = lax.optimization_barrier(part.astype(jnp.bfloat16))
    return total + low.astype(jnp.float32)

def reference(grad, weight, exp_avg, exp_avg_sq, left_basis, right_basis):
    grad_low = grad.astype(jnp.bfloat16)
    row_block = D // N_ROW
    col_block = N // N_COL

    def left_step(total, index):
        start = (index * row_block).astype(jnp.int32)
        basis_rows = lax.dynamic_slice_in_dim(left_basis, start, row_block, 0)
        grad_rows = lax.dynamic_slice_in_dim(grad_low, start, row_block, 0)
        part = lax.dot_general(basis_rows, grad_rows, (((0,), (0,)), ((), ())), preferred_element_type=jnp.float32)
        return (rounded_add(total, part), None)
    rotated_left, _ = lax.scan(left_step, jnp.zeros((D, N), jnp.float32), jnp.arange(N_ROW, dtype=jnp.int32))
    left_low = rotated_left.astype(jnp.bfloat16)

    def right_step(total, index):
        start = (index * col_block).astype(jnp.int32)
        left_cols = lax.dynamic_slice_in_dim(left_low, start, col_block, 1)
        basis_rows = lax.dynamic_slice_in_dim(right_basis, start, col_block, 0)
        part = jnp.dot(left_cols, basis_rows, preferred_element_type=jnp.float32)
        return (rounded_add(total, part), None)
    rotated, _ = lax.scan(right_step, jnp.zeros((D, N), jnp.float32), jnp.arange(N_COL, dtype=jnp.int32))
    new_avg = first_beta * exp_avg + (1.0 - first_beta) * rotated
    new_avg_sq = second_beta * exp_avg_sq + (1.0 - second_beta) * rotated * rotated
    step_low = (new_avg / first_bias / (jnp.sqrt(new_avg_sq / second_bias) + epsilon)).astype(jnp.bfloat16)
    back = lax.dot_general(step_low, right_basis, (((1,), (1,)), ((), ())), preferred_element_type=jnp.float32)
    back_low = back.astype(jnp.bfloat16)
    update = jnp.dot(left_basis, back_low, preferred_element_type=jnp.float32)
    new_weight = weight - learn_rate * (update + weight_decay * weight)
    return (new_weight, new_avg, new_avg_sq)
```

```python
import jax
import jax.numpy as jnp
import numpy as np
from jax import lax
from jax.sharding import Mesh, PartitionSpec as P

first_beta = 0.9
second_beta = 0.95
first_bias = 1.0 - 0.9**20
second_bias = 1.0 - 0.95**20
epsilon = 1e-08
learn_rate = 0.2
weight_decay = 0.1

AXES = ("y", "xl", "c", "z", "xh")
SIZES = (4, 2, 2, 4, 2)
RING = {"x": (("xl", "xh"), (0, 2, 1, 3)), "y": ("y", range(4)), "z": ("z", range(4))}
HALVES = 1
ROWS = 128 // HALVES
low = jnp.bfloat16
wide = jnp.float32


def dot(left, right, left_dim, right_dim):
    return lax.dot_general(
        left, right, (((left_dim,), (right_dim,)), ((), ())), preferred_element_type=jnp.float32
    )


def shift(value, axis, by):
    names, place = RING[axis]
    return lax.ppermute(value, names, [(place[i], place[(i + by) % 4]) for i in range(4)])


def swap(value, axis):
    return lax.ppermute(value, axis, [(0, 1), (1, 0)])


def move(value, target):
    pairs = []
    for source in range(128):
        place = target(*np.unravel_index(source, SIZES))
        pairs.append((source, int(np.ravel_multi_index(place, SIZES))))
    return lax.ppermute(value, AXES, pairs)


def gather(value, axis):
    two = shift(value, axis, 2)
    one, three = shift(value, axis, -1), shift(value, axis, 1)
    return [value, one, two, three]


def reduce(parts, axis):
    two = shift(parts[2], axis, 2)
    one, three = shift(parts[1], axis, 1), shift(parts[3], axis, -1)
    return (parts[0].astype(wide) + two.astype(wide)) + (one.astype(wide) + three.astype(wide))


def pick(test, first, second):
    return lax.select(jnp.broadcast_to(test, first.shape), first, second)


def rotate(blocks, by):
    odd, two = by % 2 == 1, by // 2 == 1
    blocks = [pick(odd, blocks[(d + 1) % 4], blocks[d]) for d in range(4)]
    return [pick(two, blocks[(d + 2) % 4], blocks[d]) for d in range(4)]


def on_device(grad, weight, exp_avg, exp_avg_sq, left_basis, right_basis):
    y, xl, c, z, xh = (lax.axis_index(name) for name in AXES)
    lo, hi = xl == 0, xh == 0

    grad_low = grad.astype(low)
    chunks = gather(grad_low, "x")
    near = pick(lo, chunks[1], chunks[3])
    far = pick(lo, chunks[3], chunks[1])
    own_cols = jnp.concatenate([chunks[0], near], axis=0)
    other_cols = jnp.concatenate([chunks[2], far], axis=0)
    grad_own = jnp.concatenate(
        [pick(hi, own_cols, other_cols), pick(hi, other_cols, own_cols)], axis=1
    )
    grad_all = jnp.concatenate([grad_own, swap(grad_own, "c")], axis=0)

    blocks = left_basis.reshape(256, 2, 2, 128)
    sub0, sub1 = blocks[:, :, 0].reshape(256, 256), blocks[:, :, 1].reshape(256, 256)
    same = move(
        pick(lo, sub0, sub1), lambda y, xl, c, z, xh: (y, xh, c, z, xl)
    )
    cross = move(
        pick(lo, sub1, sub0), lambda y, xl, c, z, xh: (y, xh, c, z, 1 - xl)
    )
    level = xl == xh
    left_part = jnp.concatenate([pick(level, same, cross), pick(level, cross, same)], axis=0)
    left_parts = rotate(gather(left_part, "z"), (y - z + 4) % 4)
    cores = [[p[:, :128] for p in left_parts], [p[:, 128:] for p in left_parts]]

    def columns(parts):
        return jnp.concatenate(
            [p[:, h * ROWS : (h + 1) * ROWS] for h in range(HALVES) for p in parts], axis=1
        )

    first, second = columns(cores[0]), columns(cores[1])
    left_own = pick(c == 0, first, second)
    left_other = pick(c == 0, second, first)
    left_tall = jnp.concatenate([left_own, swap(left_other, "c")], axis=0)

    right_part = move(right_basis, lambda y, xl, c, z, xh: (y, c, xh, z, xl))
    right_parts = rotate(gather(right_part, "y"), (z - y + 4) % 4)
    right_own = jnp.concatenate(right_parts, axis=1)
    right_other = swap(right_own, "c")
    right = jnp.concatenate(
        [pick(c == 0, right_own, right_other), pick(c == 0, right_other, right_own)], axis=0
    )

    def columns_of(array, block):
        return pick(block == 0, array[:, :384], array[:, 384:])

    def spread(array):
        own = columns_of(array, xl)
        other = swap(columns_of(array, 1 - xl), "xl")
        in_order = lo == hi
        return [
            pick(hi, own[:128], own[128:]),
            pick(in_order, other[:128], other[128:]),
            pick(hi, own[128:], own[:128]),
            pick(in_order, other[128:], other[:128]),
        ]

    avg_blocks, sq_blocks = spread(exp_avg), spread(exp_avg_sq)

    def moments(avg, avg_sq, rotated):
        new_avg = first_beta * avg + (1.0 - first_beta) * rotated
        new_avg_sq = second_beta * avg_sq + (1.0 - second_beta) * rotated * rotated
        return new_avg, new_avg_sq

    rotated_blocks = [[] for _ in range(4)]
    update = None
    for h in range(HALVES):
        span = slice(h * ROWS, (h + 1) * ROWS)
        wide_span = slice(h * 4 * ROWS, (h + 1) * 4 * ROWS)
        part = dot(left_tall[:, wide_span], grad_all, 0, 0).astype(low)
        left_low = reduce([part[d * ROWS : (d + 1) * ROWS] for d in range(4)], "y").astype(low)
        left_rows = jnp.concatenate(gather(left_low, "x"), axis=0)
        part = dot(left_rows, right, 1, 0).astype(low)
        rotated = reduce([part[:, d * 384 : (d + 1) * 384] for d in range(4)], "z")
        for d in range(4):
            rotated_blocks[d].append(rotated[d * ROWS : (d + 1) * ROWS])
        new_avg, new_avg_sq = moments(
            jnp.concatenate([b[span] for b in avg_blocks], axis=0),
            jnp.concatenate([b[span] for b in sq_blocks], axis=0),
            rotated,
        )
        step = (new_avg / first_bias / (jnp.sqrt(new_avg_sq / second_bias) + epsilon)).astype(low)
        step_rows = jnp.concatenate(gather(step, "z"), axis=1)
        part = dot(step_rows, right, 1, 1).astype(low)
        back = reduce([part[d * ROWS : (d + 1) * ROWS] for d in range(4)], "x").astype(low)
        back_own = jnp.concatenate(gather(back, "y"), axis=0)
        term = dot(left_own[:, wide_span], back_own, 1, 0)
        term = term + dot(left_other[:, wide_span], swap(back_own, "c"), 1, 0)
        update = term if update is None else update + term

    update_low = update.astype(low)

    def block(rows, test):
        strip = update_low[rows * 256 : (rows + 1) * 256]
        return pick(test, strip[:, :768], strip[:, 768:])

    straight = lo == hi
    total = reduce(
        [block(0, hi), block(1, straight), block(0, ~hi), block(1, ~straight)], "x"
    )
    new_weight = weight - learn_rate * (total + weight_decay * weight)

    rows = [jnp.concatenate(b, axis=0).astype(low) for b in rotated_blocks]
    kept = jnp.concatenate([pick(hi, rows[0], rows[2]), pick(hi, rows[2], rows[0])], axis=0)
    sent = jnp.concatenate(
        [pick(straight, rows[1], rows[3]), pick(straight, rows[3], rows[1])], axis=0
    )
    came = swap(sent, "xl")
    rotated = jnp.concatenate([pick(lo, kept, came), pick(lo, came, kept)], axis=1).astype(wide)
    new_avg, new_avg_sq = moments(exp_avg, exp_avg_sq, rotated)
    return (new_weight, new_avg, new_avg_sq)


def solution(mesh):
    grid = Mesh(np.asarray(mesh.devices).reshape(SIZES), AXES)
    row, col = ("y", "xl", "c"), ("z", "xh")
    placed = (P(row, col),) * 5 + (P(col, row),)
    return jax.shard_map(
        on_device,
        mesh=grid,
        in_specs=placed,
        out_specs=(P(row, col),) * 3,
        check_vma=False,
    )
```

```python
import jax
import jax.numpy as jnp
import numpy as np
from jax import lax
from jax.sharding import Mesh, PartitionSpec as P

first_beta = 0.9
second_beta = 0.95
first_bias = 1.0 - 0.9**20
second_bias = 1.0 - 0.95**20
epsilon = 1e-08
learn_rate = 0.2
weight_decay = 0.1

AXES = ("y", "xl", "c", "z", "xh")
SIZES = (4, 2, 2, 4, 2)
RING = {"x": (("xl", "xh"), (0, 2, 1, 3)), "y": ("y", range(4)), "z": ("z", range(4))}
HALVES = 2
ROWS = 128 // HALVES
low = jnp.bfloat16
wide = jnp.float32


def dot(left, right, left_dim, right_dim):
    return lax.dot_general(
        left, right, (((left_dim,), (right_dim,)), ((), ())), preferred_element_type=jnp.float32
    )


def shift(value, axis, by):
    names, place = RING[axis]
    return lax.ppermute(value, names, [(place[i], place[(i + by) % 4]) for i in range(4)])


def swap(value, axis):
    return lax.ppermute(value, axis, [(0, 1), (1, 0)])


def move(value, target):
    pairs = []
    for source in range(128):
        place = target(*np.unravel_index(source, SIZES))
        pairs.append((source, int(np.ravel_multi_index(place, SIZES))))
    return lax.ppermute(value, AXES, pairs)


def after(value, token):
    return lax.optimization_barrier((value, token))[0]


def near(value, axis):
    with jax.named_scope("gather_" + axis):
        return shift(value, axis, -1), shift(value, axis, 1)


def far(value, axis):
    with jax.named_scope("gather_" + axis):
        return shift(value, axis, 2)


def gather(value, axis):
    one, three = near(value, axis)
    return [value, one, far(value, axis), three]


def reduce(parts, axis):
    with jax.named_scope("reduce_" + axis):
        two = shift(parts[2], axis, 2)
        one, three = shift(parts[1], axis, 1), shift(parts[3], axis, -1)
    return (parts[0].astype(wide) + two.astype(wide)) + (one.astype(wide) + three.astype(wide))


def pick(test, first, second):
    return lax.select(jnp.broadcast_to(test, first.shape), first, second)


def turned(array):
    half = array.shape[1] // 2
    return jnp.concatenate([array[:, half:], array[:, :half]], axis=1)


def rotate(blocks, by):
    odd, two = by % 2 == 1, by // 2 == 1
    blocks = [pick(odd, blocks[(d + 1) % 4], blocks[d]) for d in range(4)]
    return [pick(two, blocks[(d + 2) % 4], blocks[d]) for d in range(4)]


def on_device(grad, weight, exp_avg, exp_avg_sq, left_basis, right_basis):
    y, xl, c, z, xh = (lax.axis_index(name) for name in AXES)
    x = 2 * xh + xl
    lo = xl == 0

    def columns_of(array, block):
        return pick(block == 0, array[:, :384], array[:, 384:])

    blocks = left_basis.reshape(256, 2, 2, 128)
    sub0, sub1 = blocks[:, :, 0].reshape(256, 256), blocks[:, :, 1].reshape(256, 256)
    left_came = swap(pick(lo, sub1, sub0), "xl")
    left_part = jnp.concatenate([pick(lo, sub0, sub1), left_came], axis=0)

    right_part = move(right_basis, lambda y, xl, c, z, xh: (y, c, xh, z, xl))

    grad_low = grad.astype(low)
    grad_near, left_near = near(grad_low, "x"), near(left_part, "z")
    grad_low, grad_near, left_part, left_near, right_part = lax.optimization_barrier(
        (grad_low, grad_near, left_part, left_near, right_part)
    )
    grad_far, left_far = far(grad_low, "x"), far(left_part, "z")
    right_near = near(right_part, "y")
    pair = jnp.concatenate([exp_avg, exp_avg_sq], axis=0)
    grad_far, left_far, right_part, right_near, pair = lax.optimization_barrier(
        (grad_far, left_far, right_part, right_near, pair)
    )
    right_far = far(right_part, "y")
    entering = swap(columns_of(pair, 1 - xl), "xl")

    beside = pick(lo, grad_near[0], grad_near[1])
    across = pick(lo, grad_near[1], grad_near[0])
    own_cols = jnp.concatenate([grad_low, beside], axis=0)
    other_cols = jnp.concatenate([grad_far, across], axis=0)
    ahead = xh == c
    grad_own = jnp.concatenate(
        [pick(ahead, own_cols, other_cols), pick(ahead, other_cols, own_cols)], axis=1
    )
    grad_other = turned(swap(grad_own, "c"))

    left_parts = rotate([left_part, left_near[0], left_far, left_near[1]], (y - z + 4) % 4)
    cores = [[p[:, :128] for p in left_parts], [p[:, 128:] for p in left_parts]]

    def columns(parts):
        return jnp.concatenate(
            [p[:, h * ROWS : (h + 1) * ROWS] for h in range(HALVES) for p in parts], axis=1
        )

    first, second = columns(cores[0]), columns(cores[1])
    left_own = pick(c == 0, first, second)
    left_other = pick(c == 0, second, first)
    left_swapped = swap(left_other, "c")

    def right_halves():
        right_chunks = [right_part, right_near[0], right_far, right_near[1]]
        right_own = jnp.concatenate(rotate(right_chunks, (z - y + 4) % 4), axis=1)
        return right_own, swap(right_own, "c")

    staying = columns_of(pair, xl)

    def spread(start):
        rows = [
            array[start + 128 * half : start + 128 * (half + 1)]
            for array in (staying, entering)
            for half in range(2)
        ]
        return rotate(rows, (4 - x) % 4)

    def moments(avg, avg_sq, rotated):
        new_avg = first_beta * avg + (1.0 - first_beta) * rotated
        new_avg_sq = second_beta * avg_sq + (1.0 - second_beta) * rotated * rotated
        return new_avg, new_avg_sq

    rotated_blocks = [[] for _ in range(4)]
    update = None
    left_lows = []
    for h in range(HALVES):
        now = slice(h * 4 * ROWS, (h + 1) * 4 * ROWS)
        part = dot(left_own[:, now], grad_own, 0, 0) + dot(left_swapped[:, now], grad_other, 0, 0)
        part = part.astype(low)
        parts = [part[d * ROWS : (d + 1) * ROWS] for d in range(4)]
        left_lows.append(reduce(parts, "y").astype(low))
    right_far, entering = after((right_far, entering), left_lows[0])
    right_own, right_other = right_halves()
    avg_blocks, sq_blocks = spread(0), spread(256)

    for h in range(HALVES):
        span = slice(h * ROWS, (h + 1) * ROWS)
        wide_span = slice(h * 4 * ROWS, (h + 1) * 4 * ROWS)
        left_low = left_lows[h]
        left_rows = jnp.concatenate(gather(left_low, "x"), axis=0)
        part = dot(left_rows[:, :768], right_own, 1, 0) + dot(left_rows[:, 768:], right_other, 1, 0)
        part = part.astype(low)
        rotated = reduce([part[:, d * 384 : (d + 1) * 384] for d in range(4)], "z")
        for d in range(4):
            rotated_blocks[d].append(rotated[d * ROWS : (d + 1) * ROWS])
        new_avg, new_avg_sq = moments(
            jnp.concatenate([b[span] for b in avg_blocks], axis=0),
            jnp.concatenate([b[span] for b in sq_blocks], axis=0),
            rotated,
        )
        step = (new_avg / first_bias / (jnp.sqrt(new_avg_sq / second_bias) + epsilon)).astype(low)
        step_rows = jnp.concatenate(gather(step, "z"), axis=1)
        part = [dot(step_rows, right, 1, 1).astype(low) for right in (right_own, right_other)]
        part = jnp.concatenate(part, axis=1)
        back = reduce([part[d * ROWS : (d + 1) * ROWS] for d in range(4)], "x").astype(low)
        back_own = jnp.concatenate(gather(back, "y"), axis=0)
        term = dot(left_own[:, wide_span], back_own, 1, 0)
        term = term + dot(left_other[:, wide_span], turned(swap(back_own, "c")), 1, 0)
        update = term if update is None else update + term

    update_low = update.astype(low)

    def block(rows, test):
        strip = update_low[rows * 256 : (rows + 1) * 256]
        return pick(test, strip[:, :768], strip[:, 768:])

    straight = lo == ahead
    total = reduce(
        [block(0, ahead), block(1, straight), block(0, ~ahead), block(1, ~straight)], "x"
    )
    new_weight = weight - learn_rate * (total + weight_decay * weight)

    rows = [jnp.concatenate(b, axis=0).astype(low) for b in rotated_blocks]
    rows = rotate(rows, x)
    kept = jnp.concatenate(rows[:2], axis=0)
    came = swap(jnp.concatenate(rows[2:], axis=0), "xl")
    rotated = jnp.concatenate([pick(lo, kept, came), pick(lo, came, kept)], axis=1).astype(wide)
    new_avg, new_avg_sq = moments(exp_avg, exp_avg_sq, rotated)
    return (new_weight, new_avg, new_avg_sq)


def solution(mesh):
    grid = Mesh(np.asarray(mesh.devices).reshape(SIZES), AXES)
    row, col = ("y", "xl", "c"), ("z", "xh")
    placed = (P(row, col),) * 5 + (P(col, row),)
    return jax.shard_map(
        on_device,
        mesh=grid,
        in_specs=placed,
        out_specs=(P(row, col),) * 3,
        check_vma=False,
    )
```

```python
import jax
import jax.numpy as jnp
import numpy as np
from jax import lax
from jax.sharding import Mesh, PartitionSpec as P

first_beta = 0.9
second_beta = 0.95
first_bias = 1.0 - 0.9**20
second_bias = 1.0 - 0.95**20
epsilon = 1e-08
learn_rate = 0.2
weight_decay = 0.1

AXES = ("y", "xl", "c", "z", "xh")
SIZES = (4, 2, 2, 4, 2)
RING = {"x": (("xl", "xh"), (0, 2, 1, 3)), "y": ("y", range(4)), "z": ("z", range(4))}
HALVES = 2
ROWS = 128 // HALVES
low = jnp.bfloat16
wide = jnp.float32


def dot(left, right, left_dim, right_dim):
    return lax.dot_general(
        left, right, (((left_dim,), (right_dim,)), ((), ())), preferred_element_type=jnp.float32
    )


def shift(value, axis, by):
    names, place = RING[axis]
    return lax.ppermute(value, names, [(place[i], place[(i + by) % 4]) for i in range(4)])


def swap(value, axis):
    return lax.ppermute(value, axis, [(0, 1), (1, 0)])


def move(value, target):
    pairs = []
    for source in range(128):
        place = target(*np.unravel_index(source, SIZES))
        pairs.append((source, int(np.ravel_multi_index(place, SIZES))))
    return lax.ppermute(value, AXES, pairs)


def after(value, token):
    return lax.optimization_barrier((value, token))[0]


def in_turn(values, token):
    return values if token is None else after(values, token)


def near(value, axis):
    with jax.named_scope("gather_" + axis):
        return shift(value, axis, -1), shift(value, axis, 1)


def far(value, axis):
    with jax.named_scope("gather_" + axis):
        return shift(value, axis, 2)


def passed_on(values, axis):
    one, three = values
    half = one.shape[0] // 2
    with jax.named_scope("gather_" + axis):
        halves = [shift(one[:half], axis, -1), shift(three[half:], axis, 1)]
    return jnp.concatenate(halves, axis=0)


def gather(value, axis, token=None):
    one, three = near(value, axis)
    return [value, one, far(value if token is None else after(value, token), axis), three]


def reduce(parts, axis, token=None):
    with jax.named_scope("reduce_" + axis):
        last = parts[2] if token is None else after(parts[2], token)
        two = shift(last, axis, 2)
        one, three = shift(parts[1], axis, 1), shift(parts[3], axis, -1)
    return (parts[0].astype(wide) + two.astype(wide)) + (one.astype(wide) + three.astype(wide))


def pick(test, first, second):
    return lax.select(jnp.broadcast_to(test, first.shape), first, second)


def turned(array):
    half = array.shape[1] // 2
    return jnp.concatenate([array[:, half:], array[:, :half]], axis=1)


def rotate(blocks, by):
    odd, two = by % 2 == 1, by // 2 == 1
    blocks = [pick(odd, blocks[(d + 1) % 4], blocks[d]) for d in range(4)]
    return [pick(two, blocks[(d + 2) % 4], blocks[d]) for d in range(4)]


def on_device(grad, weight, exp_avg, exp_avg_sq, left_basis, right_basis):
    y, xl, c, z, xh = (lax.axis_index(name) for name in AXES)
    x = 2 * xh + xl
    lo = xl == 0

    def columns_of(array, block):
        return pick(block == 0, array[:, :384], array[:, 384:])

    blocks = left_basis.reshape(256, 2, 2, 128)
    sub0, sub1 = blocks[:, :, 0].reshape(256, 256), blocks[:, :, 1].reshape(256, 256)
    left_came = swap(pick(lo, sub1, sub0), "xl")
    left_part = jnp.concatenate([pick(lo, sub0, sub1), left_came], axis=0)

    right_part = move(right_basis, lambda y, xl, c, z, xh: (y, c, xh, z, xl))

    grad_low, left_part, right_part = lax.optimization_barrier(
        (grad.astype(low), left_part, right_part)
    )
    grad_near, left_near = near(grad_low, "x"), near(left_part, "z")
    right_near = near(right_part, "y")
    grad_low, grad_near, left_part, left_near = lax.optimization_barrier(
        (grad_low, grad_near, left_part, left_near)
    )
    grad_far, left_far = far(grad_low, "x"), far(left_part, "z")
    right_far = far(after(right_part, right_near), "y")
    pair = jnp.concatenate([exp_avg, exp_avg_sq], axis=0)
    entering = swap(after(columns_of(pair, 1 - xl), grad_far), "xl")

    beside = pick(lo, grad_near[0], grad_near[1])
    across = pick(lo, grad_near[1], grad_near[0])
    own_cols = jnp.concatenate([grad_low, beside], axis=0)
    other_cols = jnp.concatenate([grad_far, across], axis=0)
    ahead = xh == c
    grad_own = jnp.concatenate(
        [pick(ahead, own_cols, other_cols), pick(ahead, other_cols, own_cols)], axis=1
    )
    grad_other = turned(swap(grad_own, "c"))

    left_parts = rotate([left_part, left_near[0], left_far, left_near[1]], (y - z + 4) % 4)
    cores = [[p[:, :128] for p in left_parts], [p[:, 128:] for p in left_parts]]

    def columns(parts):
        return jnp.concatenate(
            [p[:, h * ROWS : (h + 1) * ROWS] for h in range(HALVES) for p in parts], axis=1
        )

    first, second = columns(cores[0]), columns(cores[1])
    left_own = pick(c == 0, first, second)
    left_other = pick(c == 0, second, first)
    left_swapped = swap(left_other, "c")

    def right_halves():
        right_chunks = [right_part, right_near[0], right_far, right_near[1]]
        right_own = jnp.concatenate(rotate(right_chunks, (z - y + 4) % 4), axis=1)
        return right_own, swap(right_own, "c")

    staying = columns_of(pair, xl)

    def spread(start):
        rows = [
            array[start + 128 * half : start + 128 * (half + 1)]
            for array in (staying, entering)
            for half in range(2)
        ]
        return rotate(rows, (4 - x) % 4)

    def moments(avg, avg_sq, rotated):
        new_avg = first_beta * avg + (1.0 - first_beta) * rotated
        new_avg_sq = second_beta * avg_sq + (1.0 - second_beta) * rotated * rotated
        return new_avg, new_avg_sq

    rotated_blocks = [[None] * HALVES for _ in range(4)]
    left_lows = []
    for h in range(HALVES):
        now = slice(h * 4 * ROWS, (h + 1) * 4 * ROWS)
        part = dot(left_own[:, now], grad_own, 0, 0) + dot(left_swapped[:, now], grad_other, 0, 0)
        part = part.astype(low)
        parts = [part[d * ROWS : (d + 1) * ROWS] for d in range(4)]
        left_lows.append(reduce(parts, "y").astype(low))
    right_far, entering = after((right_far, entering), left_lows[0])
    right_own, right_other = right_halves()
    avg_blocks, sq_blocks = spread(0), spread(256)

    moved, turned_back, update = None, None, None
    tokens = {"z": None, "x": None}
    steps, backs = [None] * HALVES, [None] * HALVES
    for h in range(HALVES):
        span = slice(h * ROWS, (h + 1) * ROWS)
        left_rows = gather(left_lows[h], "x", moved)
        left_rows = jnp.concatenate(left_rows, axis=0)
        part = dot(left_rows[:, :768], right_own, 1, 0) + dot(left_rows[:, 768:], right_other, 1, 0)
        moved = part = part.astype(low)
        rotated = reduce([part[:, d * 384 : (d + 1) * 384] for d in range(4)], "z")
        for d in range(4):
            rotated_blocks[d][h] = rotated[d * ROWS : (d + 1) * ROWS]
        new_avg, new_avg_sq = moments(
            jnp.concatenate([b[span] for b in avg_blocks], axis=0),
            jnp.concatenate([b[span] for b in sq_blocks], axis=0),
            rotated,
        )
        step = new_avg / first_bias / (jnp.sqrt(new_avg_sq / second_bias) + epsilon)
        steps[h] = step.astype(low)
    for h in range(HALVES):
        step_rows = gather(steps[h], "z", turned_back)
        step_rows = jnp.concatenate(step_rows, axis=1)
        part = [dot(step_rows, right, 1, 1).astype(low) for right in (right_own, right_other)]
        turned_back = part = jnp.concatenate(part, axis=1)
        backs[h] = reduce([part[d * ROWS : (d + 1) * ROWS] for d in range(4)], "x", tokens["x"]).astype(low)
        tokens["x"] = backs[h]
    for h in range(HALVES):
        wide_span = slice(h * 4 * ROWS, (h + 1) * 4 * ROWS)
        back_own = jnp.concatenate(gather(backs[h], "y"), axis=0)
        term = dot(left_own[:, wide_span], back_own, 1, 0)
        term = term + dot(left_other[:, wide_span], turned(swap(back_own, "c")), 1, 0)
        update = term if update is None else update + term

    update_low = update.astype(low)

    def block(rows, test):
        strip = update_low[rows * 256 : (rows + 1) * 256]
        return pick(test, strip[:, :768], strip[:, 768:])

    straight = lo == ahead
    total = reduce(
        [block(0, ahead), block(1, straight), block(0, ~ahead), block(1, ~straight)], "x"
    )
    new_weight = weight - learn_rate * (total + weight_decay * weight)

    rows = [jnp.concatenate(b, axis=0).astype(low) for b in rotated_blocks]
    rows = rotate(rows, x)
    kept = jnp.concatenate(rows[:2], axis=0)
    came = swap(jnp.concatenate(rows[2:], axis=0), "xl")
    rotated = jnp.concatenate([pick(lo, kept, came), pick(lo, came, kept)], axis=1).astype(wide)
    new_avg, new_avg_sq = moments(exp_avg, exp_avg_sq, rotated)
    return (new_weight, new_avg, new_avg_sq)


def solution(mesh):
    grid = Mesh(np.asarray(mesh.devices).reshape(SIZES), AXES)
    row, col = ("y", "xl", "c"), ("z", "xh")
    placed = (P(row, col),) * 5 + (P(col, row),)
    return jax.shard_map(
        on_device,
        mesh=grid,
        in_specs=placed,
        out_specs=(P(row, col),) * 3,
        check_vma=False,
    )
```

```python
import jax
import jax.numpy as jnp
import numpy as np
from jax import lax
from jax.sharding import Mesh, PartitionSpec as P

first_beta = 0.9
second_beta = 0.95
first_bias = 1.0 - 0.9**20
second_bias = 1.0 - 0.95**20
epsilon = 1e-08
learn_rate = 0.2
weight_decay = 0.1

AXES = ("y", "xl", "c", "z", "xh")
SIZES = (4, 2, 2, 4, 2)
RING = {"x": (("xl", "xh"), (0, 2, 1, 3)), "y": ("y", range(4)), "z": ("z", range(4))}
HALVES = 2
ROWS = 128 // HALVES
low = jnp.bfloat16
wide = jnp.float32


def dot(left, right, left_dim, right_dim):
    return lax.dot_general(
        left, right, (((left_dim,), (right_dim,)), ((), ())), preferred_element_type=jnp.float32
    )


def shift(value, axis, by):
    names, place = RING[axis]
    return lax.ppermute(value, names, [(place[i], place[(i + by) % 4]) for i in range(4)])


def swap(value, axis):
    return lax.ppermute(value, axis, [(0, 1), (1, 0)])


def move(value, target):
    pairs = []
    for source in range(128):
        place = target(*np.unravel_index(source, SIZES))
        pairs.append((source, int(np.ravel_multi_index(place, SIZES))))
    return lax.ppermute(value, AXES, pairs)


def after(value, token):
    return lax.optimization_barrier((value, token))[0]


def in_turn(values, token):
    return values if token is None else after(values, token)


def near(value, axis):
    with jax.named_scope("gather_" + axis):
        return shift(value, axis, -1), shift(value, axis, 1)


def far(value, axis):
    with jax.named_scope("gather_" + axis):
        return shift(value, axis, 2)


def passed_on(values, axis):
    one, three = values
    half = one.shape[0] // 2
    with jax.named_scope("gather_" + axis):
        halves = [shift(one[:half], axis, -1), shift(three[half:], axis, 1)]
    return jnp.concatenate(halves, axis=0)


def gather(value, axis, token=None):
    one, three = near(value, axis)
    return [value, one, far(value if token is None else after(value, token), axis), three]


def reduce(parts, axis, token=None):
    with jax.named_scope("reduce_" + axis):
        last = parts[2] if token is None else after(parts[2], token)
        two = shift(last, axis, 2)
        one, three = shift(parts[1], axis, 1), shift(parts[3], axis, -1)
    return (parts[0].astype(wide) + two.astype(wide)) + (one.astype(wide) + three.astype(wide))


def pick(test, first, second):
    return lax.select(jnp.broadcast_to(test, first.shape), first, second)


def turned(array):
    half = array.shape[1] // 2
    return jnp.concatenate([array[:, half:], array[:, :half]], axis=1)


def rotate(blocks, by):
    odd, two = by % 2 == 1, by // 2 == 1
    blocks = [pick(odd, blocks[(d + 1) % 4], blocks[d]) for d in range(4)]
    return [pick(two, blocks[(d + 2) % 4], blocks[d]) for d in range(4)]


def on_device(grad, weight, exp_avg, exp_avg_sq, left_basis, right_basis):
    y, xl, c, z, xh = (lax.axis_index(name) for name in AXES)
    x = 2 * xh + xl
    lo = xl == 0

    def columns_of(array, block):
        return pick(block == 0, array[:, :384], array[:, 384:])

    blocks = left_basis.reshape(256, 2, 2, 128)
    sub0, sub1 = blocks[:, :, 0].reshape(256, 256), blocks[:, :, 1].reshape(256, 256)
    left_came = swap(pick(lo, sub1, sub0), "xl")
    left_part = jnp.concatenate([pick(lo, sub0, sub1), left_came], axis=0)

    right_part = move(right_basis, lambda y, xl, c, z, xh: (y, c, xh, z, xl))

    grad_low, left_part, right_part = lax.optimization_barrier(
        (grad.astype(low), left_part, right_part)
    )
    grad_near, left_near = near(grad_low, "x"), near(left_part, "z")
    right_near = near(right_part, "y")
    grad_low, grad_near, left_part, left_near = lax.optimization_barrier(
        (grad_low, grad_near, left_part, left_near)
    )
    grad_far, left_far = far(grad_low, "x"), far(left_part, "z")
    right_far = far(after(right_part, right_near), "y")
    pair = jnp.concatenate([exp_avg, exp_avg_sq], axis=0)
    entering = swap(after(columns_of(pair, 1 - xl), grad_far), "xl")

    beside = pick(lo, grad_near[0], grad_near[1])
    across = pick(lo, grad_near[1], grad_near[0])
    own_cols = jnp.concatenate([grad_low, beside], axis=0)
    other_cols = jnp.concatenate([grad_far, across], axis=0)
    ahead = xh == c
    grad_own = jnp.concatenate(
        [pick(ahead, own_cols, other_cols), pick(ahead, other_cols, own_cols)], axis=1
    )
    grad_other = turned(swap(grad_own, "c"))

    left_parts = rotate([left_part, left_near[0], left_far, left_near[1]], (y - z + 4) % 4)
    cores = [[p[:, :128] for p in left_parts], [p[:, 128:] for p in left_parts]]

    def columns(parts):
        return jnp.concatenate(
            [p[:, h * ROWS : (h + 1) * ROWS] for h in range(HALVES) for p in parts], axis=1
        )

    first, second = columns(cores[0]), columns(cores[1])
    left_own = pick(c == 0, first, second)
    left_other = pick(c == 0, second, first)
    left_swapped = swap(left_other, "c")

    def right_halves():
        right_chunks = [right_part, right_near[0], right_far, right_near[1]]
        right_own = jnp.concatenate(rotate(right_chunks, (z - y + 4) % 4), axis=1)
        return right_own, swap(right_own, "c")

    staying = columns_of(pair, xl)

    def spread(start):
        rows = [
            array[start + 128 * half : start + 128 * (half + 1)]
            for array in (staying, entering)
            for half in range(2)
        ]
        return rotate(rows, (4 - x) % 4)

    def moments(avg, avg_sq, rotated):
        new_avg = first_beta * avg + (1.0 - first_beta) * rotated
        new_avg_sq = second_beta * avg_sq + (1.0 - second_beta) * rotated * rotated
        return new_avg, new_avg_sq

    rotated_blocks = [[None] * HALVES for _ in range(4)]
    left_lows = []
    for h in range(HALVES):
        now = slice(h * 4 * ROWS, (h + 1) * 4 * ROWS)
        part = dot(left_own[:, now], grad_own, 0, 0) + dot(left_swapped[:, now], grad_other, 0, 0)
        part = part.astype(low)
        parts = [part[d * ROWS : (d + 1) * ROWS] for d in range(4)]
        left_lows.append(reduce(parts, "y").astype(low))
    right_far, entering = after((right_far, entering), left_lows[0])
    right_own, right_other = right_halves()
    avg_blocks, sq_blocks = spread(0), spread(256)

    moved, turned_back, update = None, None, None
    tokens = {"z": None, "x": None}
    steps, backs = [None] * HALVES, [None] * HALVES
    for h in range(HALVES):
        span = slice(h * ROWS, (h + 1) * ROWS)
        left_rows = gather(left_lows[h], "x", moved)
        left_rows = jnp.concatenate(left_rows, axis=0)
        part = dot(left_rows[:, :768], right_own, 1, 0) + dot(left_rows[:, 768:], right_other, 1, 0)
        moved = part = part.astype(low)
        rotated = reduce([part[:, d * 384 : (d + 1) * 384] for d in range(4)], "z")
        for d in range(4):
            rotated_blocks[d][h] = rotated[d * ROWS : (d + 1) * ROWS]
        new_avg, new_avg_sq = moments(
            jnp.concatenate([b[span] for b in avg_blocks], axis=0),
            jnp.concatenate([b[span] for b in sq_blocks], axis=0),
            rotated,
        )
        step = new_avg / first_bias / (jnp.sqrt(new_avg_sq / second_bias) + epsilon)
        steps[h] = step.astype(low)
    for h in range(HALVES):
        step_rows = gather(steps[h], "z", None)
        step_rows = jnp.concatenate(step_rows, axis=1)
        part = [dot(step_rows, right, 1, 1).astype(low) for right in (right_own, right_other)]
        turned_back = part = jnp.concatenate(part, axis=1)
        backs[h] = reduce([part[d * ROWS : (d + 1) * ROWS] for d in range(4)], "x", tokens["x"]).astype(low)
        tokens["x"] = backs[h]
    for h in range(HALVES):
        wide_span = slice(h * 4 * ROWS, (h + 1) * 4 * ROWS)
        back_own = jnp.concatenate(gather(backs[h], "y"), axis=0)
        term = dot(left_own[:, wide_span], back_own, 1, 0)
        term = term + dot(left_other[:, wide_span], turned(swap(back_own, "c")), 1, 0)
        update = term if update is None else update + term

    update_low = update.astype(low)

    def block(rows, test):
        strip = update_low[rows * 256 : (rows + 1) * 256]
        return pick(test, strip[:, :768], strip[:, 768:])

    straight = lo == ahead
    total = reduce(
        [block(0, ahead), block(1, straight), block(0, ~ahead), block(1, ~straight)], "x"
    )
    new_weight = weight - learn_rate * (total + weight_decay * weight)

    rows = [jnp.concatenate(b, axis=0).astype(low) for b in rotated_blocks]
    rows = rotate(rows, x)
    kept = jnp.concatenate(rows[:2], axis=0)
    came = swap(jnp.concatenate(rows[2:], axis=0), "xl")
    rotated = jnp.concatenate([pick(lo, kept, came), pick(lo, came, kept)], axis=1).astype(wide)
    new_avg, new_avg_sq = moments(exp_avg, exp_avg_sq, rotated)
    return (new_weight, new_avg, new_avg_sq)


def solution(mesh):
    grid = Mesh(np.asarray(mesh.devices).reshape(SIZES), AXES)
    row, col = ("y", "xl", "c"), ("z", "xh")
    placed = (P(row, col),) * 5 + (P(col, row),)
    return jax.shard_map(
        on_device,
        mesh=grid,
        in_specs=placed,
        out_specs=(P(row, col),) * 3,
        check_vma=False,
    )
```

```python
import jax
import jax.numpy as jnp
import numpy as np
from jax import lax
from jax.sharding import Mesh, PartitionSpec as P

first_beta = 0.9
second_beta = 0.95
first_bias = 1.0 - 0.9**20
second_bias = 1.0 - 0.95**20
epsilon = 1e-08
learn_rate = 0.2
weight_decay = 0.1

AXES = ("y", "xl", "c", "z", "xh")
SIZES = (4, 2, 2, 4, 2)
RING = {"x": (("xl", "xh"), (0, 2, 1, 3)), "y": ("y", range(4)), "z": ("z", range(4))}
HALVES = 2
ROWS = 128 // HALVES
low = jnp.bfloat16
wide = jnp.float32


def dot(left, right, left_dim, right_dim):
    return lax.dot_general(
        left, right, (((left_dim,), (right_dim,)), ((), ())), preferred_element_type=jnp.float32
    )


def shift(value, axis, by):
    names, place = RING[axis]
    return lax.ppermute(value, names, [(place[i], place[(i + by) % 4]) for i in range(4)])


def swap(value, axis):
    return lax.ppermute(value, axis, [(0, 1), (1, 0)])


def move(value, target):
    pairs = []
    for source in range(128):
        place = target(*np.unravel_index(source, SIZES))
        pairs.append((source, int(np.ravel_multi_index(place, SIZES))))
    return lax.ppermute(value, AXES, pairs)


def after(value, token):
    return lax.optimization_barrier((value, token))[0]


def in_turn(values, token):
    return values if token is None else after(values, token)


def near(value, axis):
    with jax.named_scope("gather_" + axis):
        return shift(value, axis, -1), shift(value, axis, 1)


def far(value, axis):
    with jax.named_scope("gather_" + axis):
        return shift(value, axis, 2)


def passed_on(values, axis):
    one, three = values
    half = one.shape[0] // 2
    with jax.named_scope("gather_" + axis):
        halves = [shift(one[:half], axis, -1), shift(three[half:], axis, 1)]
    return jnp.concatenate(halves, axis=0)


def gather(value, axis, token=None):
    one, three = near(value, axis)
    return [value, one, far(value if token is None else after(value, token), axis), three]


def reduce(parts, axis, token=None):
    with jax.named_scope("reduce_" + axis):
        last = parts[2] if token is None else after(parts[2], token)
        two = shift(last, axis, 2)
        one, three = shift(parts[1], axis, 1), shift(parts[3], axis, -1)
    return (parts[0].astype(wide) + two.astype(wide)) + (one.astype(wide) + three.astype(wide))


def pick(test, first, second):
    return lax.select(jnp.broadcast_to(test, first.shape), first, second)


def turned(array):
    half = array.shape[1] // 2
    return jnp.concatenate([array[:, half:], array[:, :half]], axis=1)


def rotate(blocks, by):
    odd, two = by % 2 == 1, by // 2 == 1
    blocks = [pick(odd, blocks[(d + 1) % 4], blocks[d]) for d in range(4)]
    return [pick(two, blocks[(d + 2) % 4], blocks[d]) for d in range(4)]


def on_device(grad, weight, exp_avg, exp_avg_sq, left_basis, right_basis):
    y, xl, c, z, xh = (lax.axis_index(name) for name in AXES)
    x = 2 * xh + xl
    lo = xl == 0

    def columns_of(array, block):
        return pick(block == 0, array[:, :384], array[:, 384:])

    blocks = left_basis.reshape(256, 2, 2, 128)
    sub0, sub1 = blocks[:, :, 0].reshape(256, 256), blocks[:, :, 1].reshape(256, 256)
    left_came = swap(pick(lo, sub1, sub0), "xl")
    left_part = jnp.concatenate([pick(lo, sub0, sub1), left_came], axis=0)

    right_part = move(right_basis, lambda y, xl, c, z, xh: (y, c, xh, z, xl))

    grad_low, left_part, right_part = lax.optimization_barrier(
        (grad.astype(low), left_part, right_part)
    )
    grad_near, left_near = near(grad_low, "x"), near(left_part, "z")
    right_near = near(right_part, "y")
    grad_low, grad_near, left_part, left_near = lax.optimization_barrier(
        (grad_low, grad_near, left_part, left_near)
    )
    grad_far, left_far = far(grad_low, "x"), far(left_part, "z")
    pair = jnp.concatenate([exp_avg, exp_avg_sq], axis=0)
    entering = swap(after(columns_of(pair, 1 - xl), grad_far), "xl")

    beside = pick(lo, grad_near[0], grad_near[1])
    across = pick(lo, grad_near[1], grad_near[0])
    own_cols = jnp.concatenate([grad_low, beside], axis=0)
    other_cols = jnp.concatenate([grad_far, across], axis=0)
    ahead = xh == c
    grad_own = jnp.concatenate(
        [pick(ahead, own_cols, other_cols), pick(ahead, other_cols, own_cols)], axis=1
    )
    grad_other = turned(swap(grad_own, "c"))

    left_parts = rotate([left_part, left_near[0], left_far, left_near[1]], (y - z + 4) % 4)
    cores = [[p[:, :128] for p in left_parts], [p[:, 128:] for p in left_parts]]

    def columns(parts):
        return jnp.concatenate(
            [p[:, h * ROWS : (h + 1) * ROWS] for h in range(HALVES) for p in parts], axis=1
        )

    first, second = columns(cores[0]), columns(cores[1])
    left_own = pick(c == 0, first, second)
    left_other = pick(c == 0, second, first)
    left_swapped = swap(left_other, "c")

    def right_halves():
        right_chunks = [right_part, right_near[0], right_far, right_near[1]]
        right_own = jnp.concatenate(rotate(right_chunks, (z - y + 4) % 4), axis=1)
        return right_own, swap(right_own, "c")

    staying = columns_of(pair, xl)

    def spread(start):
        rows = [
            array[start + 128 * half : start + 128 * (half + 1)]
            for array in (staying, entering)
            for half in range(2)
        ]
        return rotate(rows, (4 - x) % 4)

    def moments(avg, avg_sq, rotated):
        new_avg = first_beta * avg + (1.0 - first_beta) * rotated
        new_avg_sq = second_beta * avg_sq + (1.0 - second_beta) * rotated * rotated
        return new_avg, new_avg_sq

    rotated_blocks = [[None] * HALVES for _ in range(4)]
    left_lows = []
    for h in range(HALVES):
        now = slice(h * 4 * ROWS, (h + 1) * 4 * ROWS)
        part = dot(left_own[:, now], grad_own, 0, 0) + dot(left_swapped[:, now], grad_other, 0, 0)
        part = part.astype(low)
        if h == 0:
            right_far = far(after(right_part, (right_near, part)), "y")
        parts = [part[d * ROWS : (d + 1) * ROWS] for d in range(4)]
        left_lows.append(reduce(parts, "y").astype(low))
    right_far, entering = after((right_far, entering), left_lows[0])
    right_own, right_other = right_halves()
    avg_blocks, sq_blocks = spread(0), spread(256)

    moved, turned_back, update = None, None, None
    tokens = {"z": None, "x": None}
    steps, backs = [None] * HALVES, [None] * HALVES
    for h in range(HALVES):
        span = slice(h * ROWS, (h + 1) * ROWS)
        left_rows = gather(left_lows[h], "x", moved)
        left_rows = jnp.concatenate(left_rows, axis=0)
        part = dot(left_rows[:, :768], right_own, 1, 0) + dot(left_rows[:, 768:], right_other, 1, 0)
        moved = part = part.astype(low)
        rotated = reduce([part[:, d * 384 : (d + 1) * 384] for d in range(4)], "z")
        for d in range(4):
            rotated_blocks[d][h] = rotated[d * ROWS : (d + 1) * ROWS]
        new_avg, new_avg_sq = moments(
            jnp.concatenate([b[span] for b in avg_blocks], axis=0),
            jnp.concatenate([b[span] for b in sq_blocks], axis=0),
            rotated,
        )
        step = new_avg / first_bias / (jnp.sqrt(new_avg_sq / second_bias) + epsilon)
        steps[h] = step.astype(low)
    for h in range(HALVES):
        step_rows = gather(steps[h], "z", None)
        step_rows = jnp.concatenate(step_rows, axis=1)
        part = [dot(step_rows, right, 1, 1).astype(low) for right in (right_own, right_other)]
        turned_back = part = jnp.concatenate(part, axis=1)
        backs[h] = reduce([part[d * ROWS : (d + 1) * ROWS] for d in range(4)], "x", tokens["x"]).astype(low)
        tokens["x"] = backs[h]
    for h in range(HALVES):
        wide_span = slice(h * 4 * ROWS, (h + 1) * 4 * ROWS)
        back_own = jnp.concatenate(gather(backs[h], "y"), axis=0)
        term = dot(left_own[:, wide_span], back_own, 1, 0)
        term = term + dot(left_other[:, wide_span], turned(swap(back_own, "c")), 1, 0)
        update = term if update is None else update + term

    update_low = update.astype(low)

    def block(rows, test):
        strip = update_low[rows * 256 : (rows + 1) * 256]
        return pick(test, strip[:, :768], strip[:, 768:])

    straight = lo == ahead
    total = reduce(
        [block(0, ahead), block(1, straight), block(0, ~ahead), block(1, ~straight)], "x"
    )
    new_weight = weight - learn_rate * (total + weight_decay * weight)

    rows = [jnp.concatenate(b, axis=0).astype(low) for b in rotated_blocks]
    rows = rotate(rows, x)
    kept = jnp.concatenate(rows[:2], axis=0)
    came = swap(jnp.concatenate(rows[2:], axis=0), "xl")
    rotated = jnp.concatenate([pick(lo, kept, came), pick(lo, came, kept)], axis=1).astype(wide)
    new_avg, new_avg_sq = moments(exp_avg, exp_avg_sq, rotated)
    return (new_weight, new_avg, new_avg_sq)


def solution(mesh):
    grid = Mesh(np.asarray(mesh.devices).reshape(SIZES), AXES)
    row, col = ("y", "xl", "c"), ("z", "xh")
    placed = (P(row, col),) * 5 + (P(col, row),)
    return jax.shard_map(
        on_device,
        mesh=grid,
        in_specs=placed,
        out_specs=(P(row, col),) * 3,
        check_vma=False,
    )
```
